256 devices in a mesh: seq: 32 (over x, y, core), cb: 8 (over z).
Axes of the slice: x: 4, y: 4, z: 8, core: 2. Of those that a mesh axis runs over, the one named last changes fastest.
Arguments:
- context: bfloat16 [16384, 2048], P('seq', 'cb'), may hold values from -6 to 6
- lengths: int32 [64], replicated, may hold values from 1 to 256, 10240 in all
- tokens: int32 [16384, 8], P('seq', 'cb'), may hold values from 0 to 2047
- masks: int32 [16384, 8], P('seq', 'cb'), may hold values 0 or 1
- w_in: bfloat16 [8, 2048, 1024], P('cb', 'seq'), may hold values from -0.125 to 0.125
- w_head: bfloat16 [8, 2048, 1024], P('cb', 'seq'), may hold values from -60 to 60
Outputs:
- loss: float32 [], replicated
- grad_context: bfloat16 [16384, 2048], P('seq', 'cb')
- grad_in: float32 [8, 2048, 1024], P('cb', 'seq')
- grad_head: float32 [8, 2048, 1024], P('cb', 'seq')
The draws below stay inside these ranges and needn't reach their ends.
Inputs may be any that keep to these rules, and one draw needn't show every extreme that they name: The lengths sum to 10240, and the longest is exactly 256.
All inputs are finite; a program needn't handle non-finite values. No bound on the sum of `masks` on one device may be relied on, other than what follows from the above.
Results may differ from the reference program's by a relative error of at most 0.02.
Values may be sent and summed in bfloat16 or wider, within the bound.
No kernel may reach another device: no remote copies, remote signals or barrier semaphores. Data moves between devices by JAX's collectives and lax.ppermute only.
A program may use at most 128 MiB of HBM per device.

```python
import math
import jax
import jax.numpy as jnp
import numpy as np
from jax import lax

D = 1024
DT = 2048
V = 2048
FRAMES = 256
CB = 8
STREAMS = 64
ROWS = 16384
TOTAL_VALID = 10240


def draw_w_head(key, part):
    key = jax.random.fold_in(key, 11)
    limit = 18.0 / math.sqrt(D)
    base = jnp.clip(jax.random.normal(key, (CB, V, D), jnp.float32) * (3.0 / math.sqrt(D)), -limit, limit)
    return base.astype(jnp.bfloat16)


def with_ends(entries, rng, least, top_value):
    longest = entries.shape.index(max(entries.shape))
    spots = []
    for shift in (0, 1):
        where = [jax.random.randint(jax.random.fold_in(rng, axis), (), 0, length) for axis, length in enumerate(entries.shape)]
        where[longest] = (where[longest] + shift) % entries.shape[longest]
        spots.append(tuple(where))
    return entries.at[spots[0]].set(least).at[spots[1]].set(top_value)


def steps_of(key, shape, pieces, low, high):
    def one(axis_at, shards_of):
        draws = jax.random.uniform(jax.random.fold_in(jax.random.fold_in(key, 6), axis_at), (shards_of,), jnp.float32, low / len(pieces), high / len(pieces))
        return jnp.repeat(jnp.exp(draws), shape[axis_at] // shards_of).reshape((-1,) + (1,) * (len(shape) - axis_at - 1))

    gain = one(*pieces[0])
    for cut in pieces[1:]:
        gain = gain * one(*cut)
    return gain


def split_up(number_of, total, bound, slope):
    weights = [(1 << 20) // math.isqrt(grade ** slope) + 1 for grade in range(2, number_of + 1)]
    surplus, holding = total - bound - (number_of - 1), [1] * (number_of - 1)
    while surplus > 0:
        movable = [i for i in range(number_of - 1) if holding[i] < bound]
        mass, remaining = sum([weights[i] for i in movable]), surplus
        for i in movable:
            extra = min(bound - holding[i], max(1, remaining * weights[i] // mass), surplus)
            holding[i] = holding[i] + extra
            surplus = surplus - extra
    return np.array([bound] + holding)


def ragged(key, count, total, bound, lean):
    if count == 2:
        one = jax.random.randint(key, (), max(1, total - bound), min(bound, total - 1) + 1)
        return jnp.stack([one, total - one])
    sizes = jnp.asarray(split_up(count, total, bound, lean), jnp.int32)
    pairs = (count - 1) // 2
    source_of, taker = sizes[1:1 + 2 * pairs:2], sizes[2:2 + 2 * pairs:2]
    slack = jnp.minimum(source_of - 1, bound - taker)
    passed = jax.random.randint(jax.random.fold_in(key, 1), (pairs,), 0, 1 << 20) % (slack + 1)
    sizes = sizes.at[1:1 + 2 * pairs:2].set(source_of - passed).at[2:2 + 2 * pairs:2].set(taker + passed)
    return sizes[jax.random.permutation(jax.random.fold_in(key, 2), count)]


def scatter_about(rng, shape, spread, most, split=(), kind=jnp.bfloat16):
    entries = jax.random.normal(rng, shape, jnp.float32) * spread
    if len(split) > 0:
        entries = steps_of(rng, shape, split, -0.22, 0.18) * entries
    return jnp.clip(entries, min=-most, max=most).astype(kind)


def setup_inputs(seed: int = 0) -> dict:
    seeds = jax.random.split(jax.random.key(seed), 7)
    context = scatter_about(seeds[0], (ROWS, DT), 1.0, 6.0, ((0, 32), (1, 8)))
    lengths = ragged(seeds[1], STREAMS, TOTAL_VALID, FRAMES, 2).astype(jnp.int32)
    tokens = with_ends(jax.random.randint(seeds[2], (ROWS, CB), 0, V), jax.random.fold_in(seeds[2], 1), 0, V - 1).astype(jnp.int32)
    masks = with_ends((jax.random.randint(seeds[3], (ROWS, CB), 0, 8) < 7).astype(jnp.int32), jax.random.fold_in(seeds[3], 1), 0, 1)
    w_in = scatter_about(seeds[4], (CB, DT, D), DT ** -0.5, 0.125, ((0, 8), (1, 32)))
    w_head = draw_w_head(jax.random.fold_in(seeds[6], 71), 0)
    return {"context": context, "lengths": lengths, "tokens": tokens, "masks": masks, "w_in": w_in, "w_head": w_head}


EPS = 1e-06

def reference(context, lengths, tokens, masks, w_in, w_head):
    positions = jnp.arange(ROWS, dtype=jnp.int32)
    live = positions % FRAMES < lengths[positions // FRAMES]
    use = live[:, None] & (masks > 0)
    counts = lax.optimization_barrier(jnp.sum(use.astype(jnp.float32), axis=0))
    vocab_ids = jnp.arange(V, dtype=jnp.int32)
    loss = jnp.float32(0.0)
    grad_context = jnp.zeros((ROWS, DT), jnp.float32)
    grads_in = []
    grads_head = []
    for code in range(CB):
        hidden = jnp.dot(context, w_in[code], preferred_element_type=jnp.float32)
        inverse = lax.rsqrt(lax.optimization_barrier(jnp.mean(hidden * hidden, axis=1, keepdims=True)) + EPS)
        normed = hidden * inverse
        normed_bf = normed.astype(jnp.bfloat16)
        logits = lax.dot_general(normed_bf, w_head[code], (((1,), (1,)), ((), ())), preferred_element_type=jnp.float32)
        peak = lax.optimization_barrier(jnp.max(logits, axis=1, keepdims=True))
        shifted = jnp.exp(logits - peak)
        total = lax.optimization_barrier(jnp.sum(shifted, axis=1, keepdims=True))
        target = vocab_ids[None, :] == tokens[:, code:code + 1]
        picked = lax.optimization_barrier(jnp.sum(jnp.where(target, logits, 0.0), axis=1))
        keeps = use[:, code]
        entropy_terms = jnp.where(keeps, peak[:, 0] + jnp.log(total[:, 0]) - picked, 0.0)
        loss = loss + jnp.sum(entropy_terms) / counts[code] / CB
        weight = keeps.astype(jnp.float32) * (ROWS / (counts[code] * CB))
        grad_logits = ((shifted / total - target.astype(jnp.float32)) * weight[:, None]).astype(jnp.bfloat16)
        grads_head.append(lax.dot_general(grad_logits, normed_bf, (((0,), (0,)), ((), ())), preferred_element_type=jnp.float32))
        grad_normed = jnp.dot(grad_logits, w_head[code], preferred_element_type=jnp.float32)
        grad_hidden = inverse * (grad_normed - normed * lax.optimization_barrier(jnp.mean(grad_normed * normed, axis=1, keepdims=True)))
        grad_hidden_bf = grad_hidden.astype(jnp.bfloat16)
        grads_in.append(lax.dot_general(context, grad_hidden_bf, (((0,), (0,)), ((), ())), preferred_element_type=jnp.float32))
        grad_context = grad_context + lax.dot_general(grad_hidden_bf, w_in[code], (((1,), (1,)), ((), ())), preferred_element_type=jnp.float32)
    return (loss, grad_context.astype(jnp.bfloat16), jnp.stack(grads_in), jnp.stack(grads_head))
```

```python
import jax
import jax.numpy as jnp
from jax import lax
from jax.sharding import PartitionSpec as P

FRAMES = 256
EPS = 1e-06
BF = jnp.bfloat16
F32 = jnp.float32
NX, NY, NC, NZ = 4, 4, 2, 8


def seq_index(x, y, c):
    return (x * NY + y) * NC + c


def shift_x(k):
    return [
        (seq_index(x, y, c), seq_index((x + k) % NX, y, c))
        for x in range(NX) for y in range(NY) for c in range(NC)
    ]


def shift_y(k):
    return [
        (seq_index(x, y, c), seq_index(x, (y + k) % NY, c))
        for x in range(NX) for y in range(NY) for c in range(NC)
    ]


def swap_core():
    return [(i, i ^ 1) for i in range(NX * NY * NC)]


def shift_z(k):
    return [(i, (i + k) % NZ) for i in range(NZ)]


def lookup(table, index):
    spots = jnp.arange(table.shape[0], dtype=jnp.int32)
    return jnp.sum(jnp.where(index[:, None] == spots[None, :], table[None, :], 0), axis=1)


def gather_z(block):
    z = lax.axis_index("cb")
    width = block.shape[1]
    full = jnp.zeros((block.shape[0], NZ * width), block.dtype)
    full = lax.dynamic_update_slice(full, block, (0, z * width))
    for k in (4, 3, -3, 2, -2, 1, -1):
        piece = lax.ppermute(block, "cb", shift_z(k))
        full = lax.dynamic_update_slice(full, piece, (0, ((z - k) % NZ) * width))
    return full


def pick(array, index):
    return lax.dynamic_index_in_dim(array, index, 0, keepdims=False)


def scatter_axis(blocks, here, count, shift):
    total = pick(blocks, here).astype(F32)
    for k in (2, 1, 3):
        piece = lax.ppermute(pick(blocks, (here + k) % count), "seq", shift(k))
        total = total + piece.astype(F32)
    return total


def scatter_seq(term, x_first):
    here = lax.axis_index("seq")
    c, y, x = here % NC, (here // NC) % NY, here // (NC * NY)
    rows = term.shape[0] // (NX * NY * NC)
    blocks = term.reshape(NX, NY, NC, rows, -1)
    core_first = jnp.moveaxis(blocks, 2, 0)
    other = lax.ppermute(pick(core_first, 1 - c), "seq", swap_core())
    both = (pick(core_first, c).astype(F32) + other.astype(F32)).astype(BF)
    if x_first:
        part = scatter_axis(both, x, NX, shift_x).astype(BF)
        return scatter_axis(part, y, NY, shift_y)
    part = scatter_axis(jnp.moveaxis(both, 1, 0), y, NY, shift_y).astype(BF)
    return scatter_axis(part, x, NX, shift_x)


def sum_everywhere(value):
    tile = jnp.full((8, 128), value, F32)
    tile = tile + lax.ppermute(tile, "seq", swap_core())
    for k in (1, 2):
        tile = tile + lax.ppermute(tile, "seq", shift_x(k))
    for k in (1, 2):
        tile = tile + lax.ppermute(tile, "seq", shift_y(k))
    for k in (1, 2, 4):
        tile = tile + lax.ppermute(tile, "cb", shift_z(k))
    return tile[0, 0]


def local(context, lengths, tokens, masks, w_in, w_head):
    seq_count = lax.axis_size("seq")
    cb_total = lax.axis_size("cb") * w_in.shape[0]
    seq_here = lax.axis_index("seq")
    rows_here = context.shape[0]
    streams_here = rows_here // FRAMES
    width = w_in.shape[2]
    pair = lax.all_gather(jnp.concatenate([w_in[0], w_head[0]], axis=1), "seq", axis=0, tiled=True)

    positions = jnp.arange(rows_here, dtype=jnp.int32)
    own_stream = seq_here * streams_here + positions // FRAMES
    live = positions % FRAMES < lookup(lengths, own_stream)
    labels = jnp.where(live & (masks[:, 0] > 0), tokens[:, 0], -1)
    keeps = labels >= 0
    keep_float = keeps.astype(F32)
    tally = jnp.concatenate([keep_float, jnp.zeros((1024 - rows_here,), F32)]).reshape(8, 128)
    count = jnp.sum(lax.all_gather(tally, "seq", axis=0))
    full_rows = gather_z(context)
    full_rows, count, pair = lax.optimization_barrier((full_rows, count, pair))

    in_matrix = pair[:, :width]
    head_matrix = pair[:, width:]
    hidden = jnp.dot(full_rows, in_matrix, preferred_element_type=F32)
    inverse = lax.rsqrt(jnp.mean(hidden * hidden, axis=1, keepdims=True) + EPS)
    normed = hidden * inverse
    normed_bf = normed.astype(BF)
    logits = lax.dot_general(
        normed_bf, head_matrix, (((1,), (1,)), ((), ())), preferred_element_type=F32
    )
    peak = jnp.max(logits, axis=1, keepdims=True)
    shifted = jnp.exp(logits - peak)
    total = jnp.sum(shifted, axis=1, keepdims=True)
    vocab_ids = jnp.arange(logits.shape[1], dtype=jnp.int32)
    target = vocab_ids[None, :] == labels[:, None]
    picked = jnp.sum(jnp.where(target, logits, 0.0), axis=1)
    entropy_terms = jnp.where(keeps, peak[:, 0] + jnp.log(total[:, 0]) - picked, 0.0)
    rows_total = FRAMES * streams_here * seq_count
    weight = keep_float * (rows_total / (count * cb_total))
    grad_logits = ((shifted / total - target.astype(F32)) * weight[:, None]).astype(BF)
    head_term = lax.dot_general(
        grad_logits, normed_bf, (((0,), (0,)), ((), ())), preferred_element_type=F32
    ).astype(BF)
    head_part = scatter_seq(head_term, True)
    grad_normed = jnp.dot(grad_logits, head_matrix, preferred_element_type=F32)
    grad_hidden = inverse * (
        grad_normed - normed * jnp.mean(grad_normed * normed, axis=1, keepdims=True)
    )
    grad_hidden_bf = grad_hidden.astype(BF)
    context_term = lax.dot_general(
        grad_hidden_bf, in_matrix, (((1,), (1,)), ((), ())), preferred_element_type=F32
    ).astype(BF)
    context_part = lax.psum_scatter(context_term, "cb", scatter_dimension=1, tiled=True)
    in_term = lax.dot_general(
        full_rows, grad_hidden_bf, (((0,), (0,)), ((), ())), preferred_element_type=F32
    ).astype(BF)
    in_part = scatter_seq(in_term, False)
    loss = sum_everywhere(jnp.sum(entropy_terms) / count / cb_total)
    return (loss, context_part, in_part[None], head_part[None])


def solution(mesh):
    in_specs = (
        P("seq", "cb"),
        P(),
        P("seq", "cb"),
        P("seq", "cb"),
        P("cb", "seq", None),
        P("cb", "seq", None),
    )
    out_specs = (P(), P("seq", "cb"), P("cb", "seq", None), P("cb", "seq", None))
    return jax.shard_map(local, mesh=mesh, in_specs=in_specs, out_specs=out_specs, check_vma=False)
```

```python
import jax
import jax.numpy as jnp
from jax import lax
from jax.experimental import pallas as pl
from jax.experimental.pallas import tpu as pltpu
from jax.sharding import PartitionSpec as P

FRAMES = 256
EPS = 1e-06
BF = jnp.bfloat16
F32 = jnp.float32
NX, NY, NC, NZ = 4, 4, 2, 8
TILE = 256
VMEM_LIMIT = 50 * 1024 * 1024


def seq_index(x, y, c):
    return (x * NY + y) * NC + c


def moves(step):
    pairs = []
    for x in range(NX):
        for y in range(NY):
            for c in range(NC):
                to_x, to_y, to_c = step(x, y, c)
                pairs.append((seq_index(x, y, c), seq_index(to_x % NX, to_y % NY, to_c)))
    return pairs


def shift_x(k):
    return moves(lambda x, y, c: (x + k, y, c))


def shift_y(k):
    return moves(lambda x, y, c: (x, y + k, c))


def lane_x(k):
    return moves(lambda x, y, c: (x + k * (1 - 2 * c), y, c))


def lane_y(k):
    return moves(lambda x, y, c: (x, y + k * (1 - 2 * c), c))


def swap_core():
    return moves(lambda x, y, c: (x, y, 1 - c))


def shift_z(k):
    return [(i, (i + k) % NZ) for i in range(NZ)]


def lookup(table, index):
    spots = jnp.arange(table.shape[0], dtype=jnp.int32)
    return jnp.sum(jnp.where(index[:, None] == spots[None, :], table[None, :], 0), axis=1)


def together(*values):
    return lax.optimization_barrier(values)


def gather_z(block):
    z = lax.axis_index("cb")
    width = block.shape[1]
    full = jnp.zeros((block.shape[0], NZ * width), block.dtype)
    full = lax.dynamic_update_slice(full, block, (0, z * width))
    for k in (4, 3, -3, 2, -2, 1, -1):
        piece = lax.ppermute(block, "cb", shift_z(k))
        full = lax.dynamic_update_slice(full, piece, (0, ((z - k) % NZ) * width))
    return full


def dot(a, b, dims):
    return lax.dot_general(a, b, (dims, ((), ())), preferred_element_type=F32)


def forward_body(
    core, rows, labels, weight, keeps, pair, pair_blocks,
    normed, normed_bf, inverse, grad_keep, grad_send, entropy,
    w_in, w_head, logits, sems,
):
    c = core[0]
    n_rows, width = normed.shape
    vocab = logits.shape[1]
    half = vocab // 2
    load_in = pltpu.make_async_copy(pair.at[:, pl.ds(0, width)], w_in, sems.at[0])
    load_in.start()
    loads = []
    for part in range(NC):
        parity = jnp.bitwise_xor(c, part)
        for y in range(NY):
            copy = pltpu.make_async_copy(
                pair_blocks.at[:, y, parity, :, pl.ds(width, width)],
                w_head.at[part, y],
                sems.at[1 + part * NY + y],
            )
            copy.start()
            loads.append(copy)
    load_in.wait()

    def hidden_tile(n, squares):
        cols = pl.ds(pl.multiple_of(n * TILE, TILE), TILE)
        tile = dot(rows[...], w_in[:, cols], ((1,), (0,)))
        normed[:, cols] = tile
        return squares + jnp.sum(tile * tile, axis=1, keepdims=True)

    squares = lax.fori_loop(0, width // TILE, hidden_tile, jnp.zeros((n_rows, 1), F32))
    inv = lax.rsqrt(squares / width + EPS)
    inverse[...] = inv
    for n in range(width // TILE):
        cols = pl.ds(n * TILE, TILE)
        tile = normed[:, cols] * inv
        normed[:, cols] = tile
        normed_bf[:, cols] = tile.astype(BF)
    for copy in loads:
        copy.wait()

    def logits_tile(n, peak):
        part, y = n // NY, n % NY
        block = w_head[part, y].reshape(TILE, width)
        tile = dot(normed_bf[...], block, ((1,), (1,)))
        logits[:, pl.ds(pl.multiple_of(n * TILE, TILE), TILE)] = tile
        return jnp.maximum(peak, jnp.max(tile, axis=1, keepdims=True))

    tiles = vocab // TILE
    peak = lax.fori_loop(0, tiles, logits_tile, jnp.full((n_rows, 1), -jnp.inf, F32))
    label = labels[...]
    spots = lax.broadcasted_iota(jnp.int32, (n_rows, TILE), 1)

    def exp_tile(n, carry):
        total, picked = carry
        cols = pl.ds(pl.multiple_of(n * TILE, TILE), TILE)
        tile = logits[:, cols]
        picked = picked + jnp.sum(
            jnp.where(spots == label - n * TILE, tile, 0.0), axis=1, keepdims=True
        )
        tile = jnp.exp(tile - peak)
        logits[:, cols] = tile
        return total + jnp.sum(tile, axis=1, keepdims=True), picked

    zero = jnp.zeros((n_rows, 1), F32)
    total, picked = lax.fori_loop(0, tiles, exp_tile, (zero, zero))
    entropy[...] = jnp.where(keeps[...] > 0, peak + jnp.log(total) - picked, 0.0)
    scale = weight[...] / total
    flat = weight[...]

    def grad_tile(n, out, offset):
        cols = pl.ds(pl.multiple_of(n * TILE, TILE), TILE)
        from_cols = pl.ds(pl.multiple_of(n * TILE + offset, TILE), TILE)
        hit = spots == label - (n * TILE + offset)
        out[:, cols] = (logits[:, from_cols] * scale - jnp.where(hit, flat, 0.0)).astype(BF)

    def keep_tile(n, _):
        grad_tile(n, grad_keep, 0)
        return _

    def send_tile(n, _):
        grad_tile(n, grad_send, half)
        return _

    lax.fori_loop(0, half // TILE, keep_tile, 0)
    lax.fori_loop(0, half // TILE, send_tile, 0)


def forward(core, rows, labels, weight, keeps, pair):
    n_rows = rows.shape[0]
    deep, both = pair.shape
    width = both // 2
    vocab = deep
    block_rows = deep // (NX * NY * NC)
    whole = pl.BlockSpec(memory_space=pltpu.VMEM)
    return pl.pallas_call(
        forward_body,
        out_shape=[
            jax.ShapeDtypeStruct((n_rows, width), F32),
            jax.ShapeDtypeStruct((n_rows, width), BF),
            jax.ShapeDtypeStruct((n_rows, 1), F32),
            jax.ShapeDtypeStruct((n_rows, vocab // 2), BF),
            jax.ShapeDtypeStruct((n_rows, vocab // 2), BF),
            jax.ShapeDtypeStruct((n_rows, 1), F32),
        ],
        in_specs=[pl.BlockSpec(memory_space=pltpu.SMEM)] + [whole] * 4
        + [pl.BlockSpec(memory_space=pl.ANY)] * 2,
        out_specs=[whole] * 6,
        scratch_shapes=[
            pltpu.VMEM((deep, width), BF),
            pltpu.VMEM((NC, NY, NX, block_rows, width), BF),
            pltpu.VMEM((n_rows, vocab), F32),
            pltpu.SemaphoreType.DMA((1 + NC * NY,)),
        ],
        compiler_params=pltpu.CompilerParams(vmem_limit_bytes=VMEM_LIMIT),
        cost_estimate=pl.CostEstimate(
            flops=4 * n_rows * deep * width, bytes_accessed=16 << 20, transcendentals=n_rows * vocab
        ),
        name="forward_rows",
    )(core, rows, labels, weight, keeps, pair, pair.reshape(NX, NY, NC, block_rows, both))


def hidden_grad_body(
    core, grad_keep, grad_send, normed, inverse, pair_blocks, out, w_head, grad, sems
):
    c = core[0]
    n_rows, width = normed.shape
    half = grad_keep.shape[1]
    loads = []
    for part in range(NC):
        parity = jnp.bitwise_xor(c, part)
        for y in range(NY):
            copy = pltpu.make_async_copy(
                pair_blocks.at[:, y, parity, :, pl.ds(width, width)],
                w_head.at[part, y],
                sems.at[part * NY + y],
            )
            copy.start()
            loads.append(copy)
    for copy in loads:
        copy.wait()

    def grad_tile(n, mean):
        cols = pl.ds(pl.multiple_of(n * TILE, TILE), TILE)
        tile = dot(grad_keep[...], w_head[0, :, :, :, cols].reshape(half, TILE), ((1,), (0,)))
        tile += dot(grad_send[...], w_head[1, :, :, :, cols].reshape(half, TILE), ((1,), (0,)))
        grad[:, cols] = tile
        return mean + jnp.sum(tile * normed[:, cols], axis=1, keepdims=True)

    mean = lax.fori_loop(0, width // TILE, grad_tile, jnp.zeros((n_rows, 1), F32)) / width
    inv = inverse[...]
    for n in range(width // TILE):
        cols = pl.ds(n * TILE, TILE)
        out[:, cols] = (inv * (grad[:, cols] - normed[:, cols] * mean)).astype(BF)


def hidden_grad(core, grad_keep, grad_send, normed, inverse, pair):
    n_rows, width = normed.shape
    deep, both = pair.shape
    block_rows = deep // (NX * NY * NC)
    whole = pl.BlockSpec(memory_space=pltpu.VMEM)
    return pl.pallas_call(
        hidden_grad_body,
        out_shape=jax.ShapeDtypeStruct((n_rows, width), BF),
        in_specs=[pl.BlockSpec(memory_space=pltpu.SMEM)] + [whole] * 4
        + [pl.BlockSpec(memory_space=pl.ANY)],
        out_specs=whole,
        scratch_shapes=[
            pltpu.VMEM((NC, NY, NX, block_rows, width), BF),
            pltpu.VMEM((n_rows, width), F32),
            pltpu.SemaphoreType.DMA((NC * NY,)),
        ],
        compiler_params=pltpu.CompilerParams(vmem_limit_bytes=VMEM_LIMIT),
        cost_estimate=pl.CostEstimate(
            flops=2 * n_rows * deep * width, bytes_accessed=10 << 20, transcendentals=0
        ),
        name="hidden_grad",
    )(core, grad_keep, grad_send, normed, inverse, pair.reshape(NX, NY, NC, block_rows, both))


def weight_grad_body(order, a_here, a_there, b_here, b_there, *rest):
    outs, (turned_here, turned_there) = rest[:4], rest[4:]
    block = outs[0].shape[0]
    width = b_here.shape[1]
    for j in range(4):
        cols = pl.ds(pl.multiple_of(order[j] * block, block), block)
        turned_here[j * block : (j + 1) * block, :] = a_here[:, cols].T
        turned_there[j * block : (j + 1) * block, :] = a_there[:, cols].T

    def tile_step(n, _):
        cols = pl.ds(pl.multiple_of(n * TILE, TILE), TILE)
        tile = dot(turned_here[...], b_here[:, cols], ((1,), (0,)))
        tile += dot(turned_there[...], b_there[:, cols], ((1,), (0,)))
        for j in range(4):
            outs[j][:, cols] = tile[j * block : (j + 1) * block].astype(outs[j].dtype)
        return _

    lax.fori_loop(0, width // TILE, tile_step, 0)


def weight_grad(order, a_here, a_there, b_here, b_there):
    n_rows, deep = a_here.shape
    width = b_here.shape[1]
    block = deep // 4
    whole = pl.BlockSpec(memory_space=pltpu.VMEM)
    return pl.pallas_call(
        weight_grad_body,
        out_shape=[jax.ShapeDtypeStruct((block, width), t) for t in (BF, BF, F32, F32)],
        in_specs=[pl.BlockSpec(memory_space=pltpu.SMEM)] + [whole] * 4,
        out_specs=[whole] * 4,
        scratch_shapes=[pltpu.VMEM((deep, n_rows), BF)] * 2,
        compiler_params=pltpu.CompilerParams(vmem_limit_bytes=VMEM_LIMIT),
        cost_estimate=pl.CostEstimate(
            flops=4 * n_rows * deep * width, bytes_accessed=8 << 20, transcendentals=0
        ),
        name="weight_grad",
    )(order, a_here, a_there, b_here, b_there)


def send_order(here, c, count):
    way = 1 - 2 * c
    return jnp.stack(
        [(here + 2) % count, (here - way) % count, (here + way) % count, here]
    ).astype(jnp.int32)


def first_stage(blocks, lane):
    relay, against, along, mine = blocks
    passing = lax.ppermute(relay, "seq", lane(1))
    direct = lax.ppermute(against, "seq", lane(-1))
    merged = (along + passing.astype(F32)).astype(BF)
    last = lax.ppermute(merged, "seq", lane(1))
    return mine + direct.astype(F32) + last.astype(F32)


def second_stage(part, here, count, shift):
    width = part.shape[1]
    blocks = part.reshape(count, -1, width)
    total = lax.dynamic_index_in_dim(blocks, here, 0, keepdims=False)
    small = blocks.astype(BF)
    for k in (2, 1, 3):
        piece = lax.dynamic_index_in_dim(small, (here + k) % count, 0, keepdims=False)
        total = total + lax.ppermute(piece, "seq", shift(k)).astype(F32)
    return total


def local(context, lengths, tokens, masks, w_in, w_head):
    seq_count = lax.axis_size("seq")
    cb_total = lax.axis_size("cb") * w_in.shape[0]
    seq_here = lax.axis_index("seq")
    c, y, x = seq_here % NC, (seq_here // NC) % NY, seq_here // (NC * NY)
    core = jnp.reshape(c, (1,)).astype(jnp.int32)
    rows_here, slab = context.shape
    streams_here = rows_here // FRAMES
    w_rows, width = w_in.shape[1:]
    vocab = w_rows * seq_count
    pair = lax.all_gather(jnp.concatenate([w_in[0], w_head[0]], axis=1), "seq", axis=0, tiled=True)

    positions = jnp.arange(rows_here, dtype=jnp.int32)
    own_stream = seq_here * streams_here + positions // FRAMES
    live = positions % FRAMES < lookup(lengths, own_stream)
    keeps = live & (masks[:, 0] > 0)
    keep_float = keeps.astype(F32)
    token = tokens[:, 0]
    owner, spot = token // w_rows, token % w_rows
    own_x, own_y, own_c = owner // (NY * NC), (owner // NC) % NY, owner % NC
    column = ((((own_c + c) % NC) * NY + own_y) * NX + own_x) * w_rows + spot
    labels = jnp.where(keeps, column, -1)
    tally = jnp.concatenate([keep_float, jnp.zeros((1024 - rows_here,), F32)]).reshape(8, 128)
    count = jnp.sum(lax.all_gather(tally, "seq", axis=0))
    rows_total = FRAMES * streams_here * seq_count
    weight = keep_float * (rows_total / (count * cb_total))

    full_rows = gather_z(context)
    by_core = full_rows.reshape(rows_here, NX * NY, NC, w_rows)
    even = by_core[:, :, 0].reshape(rows_here, -1)
    odd = by_core[:, :, 1].reshape(rows_here, -1)
    rows_keep = jnp.where(c == 0, even, odd)
    rows_other = lax.ppermute(jnp.where(c == 0, odd, even), "seq", swap_core())
    full_rows, weight, rows_keep, rows_other, pair = together(
        full_rows, weight, rows_keep, rows_other, pair
    )

    normed, normed_bf, inverse, grad_keep, grad_send, entropy = forward(
        core, full_rows, labels[:, None], weight[:, None], keep_float[:, None], pair
    )
    grad_other = lax.ppermute(grad_send, "seq", swap_core())
    normed_other = lax.ppermute(normed_bf, "seq", swap_core())
    tile = jnp.full((8, 128), jnp.sum(entropy) / count / cb_total, F32)
    tile_in = lax.ppermute(tile, "seq", swap_core())
    grad_hidden = hidden_grad(core, grad_keep, grad_send, normed, inverse, pair)
    grad_hidden, tile, tile_in = together(grad_hidden, tile, tile_in)
    hidden_other = lax.ppermute(grad_hidden, "seq", swap_core())
    tile = tile + tile_in
    tile_in = lax.ppermute(tile, "cb", shift_z(1))
    context_term = dot(grad_hidden, pair[:, :width], ((1,), (1,))).astype(BF)
    grad_other, normed_other, context_term, tile, tile_in = together(
        grad_other, normed_other, context_term, tile, tile_in
    )
    context_part = lax.psum_scatter(context_term, "cb", scatter_dimension=1, tiled=True)
    tile = tile + tile_in
    tile_in = lax.ppermute(tile, "cb", shift_z(2))
    head_blocks = weight_grad(send_order(y, c, NY), grad_keep, grad_other, normed_bf, normed_other)
    head_blocks, hidden_other, tile, tile_in = together(head_blocks, hidden_other, tile, tile_in)
    tile = tile + tile_in
    tile_in = lax.ppermute(tile, "cb", shift_z(4))
    head_sum = first_stage(head_blocks, lane_y)
    in_blocks = weight_grad(send_order(x, c, NX), rows_keep, rows_other, grad_hidden, hidden_other)
    in_blocks, tile, tile_in = together(in_blocks, tile, tile_in)
    in_sum = first_stage(in_blocks, lane_x)
    tile = tile + tile_in
    tile = tile + lax.ppermute(tile, "seq", shift_x(1))
    tile = tile + lax.ppermute(tile, "seq", shift_x(2))
    tile = tile + lax.ppermute(tile, "seq", shift_y(1))
    tile = tile + lax.ppermute(tile, "seq", shift_y(2))
    head_part = second_stage(head_sum, x, NX, shift_x)
    in_part = second_stage(in_sum, y, NY, shift_y)
    return (tile[0, 0], context_part, in_part[None], head_part[None])


def solution(mesh):
    in_specs = (
        P("seq", "cb"),
        P(),
        P("seq", "cb"),
        P("seq", "cb"),
        P("cb", "seq", None),
        P("cb", "seq", None),
    )
    out_specs = (P(), P("seq", "cb"), P("cb", "seq", None), P("cb", "seq", None))
    return jax.shard_map(local, mesh=mesh, in_specs=in_specs, out_specs=out_specs, check_vma=False)
```

```python
import functools

import jax
import jax.numpy as jnp
from jax import lax
from jax.experimental import pallas as pl
from jax.experimental.pallas import tpu as pltpu
from jax.sharding import PartitionSpec as P

FRAMES = 256
EPS = 1e-06
BF = jnp.bfloat16
F32 = jnp.float32
NX, NY, NC, NZ = 4, 4, 2, 8
EXTRA = 16
VMEM_LIMIT = 40 * 1024 * 1024


def seq_index(x, y, c):
    return (x * NY + y) * NC + c


def moves(step):
    pairs = []
    for x in range(NX):
        for y in range(NY):
            for c in range(NC):
                to_x, to_y, to_c = step(x, y, c)
                pairs.append((seq_index(x, y, c), seq_index(to_x % NX, to_y % NY, to_c)))
    return pairs


def shift_x(k):
    return moves(lambda x, y, c: (x + k, y, c))


def shift_y(k):
    return moves(lambda x, y, c: (x, y + k, c))


def lane_x(k):
    return moves(lambda x, y, c: (x + k * (1 - 2 * c), y, c))


def lane_y(k):
    return moves(lambda x, y, c: (x, y + k * (1 - 2 * c), c))


def swap_core():
    return moves(lambda x, y, c: (x, y, 1 - c))


def shift_z(k):
    return [(i, (i + k) % NZ) for i in range(NZ)]


def lookup(table, index):
    spots = jnp.arange(table.shape[0], dtype=jnp.int32)
    return jnp.sum(jnp.where(index[:, None] == spots[None, :], table[None, :], 0), axis=1)


def together(*values):
    return lax.optimization_barrier(values)


def dot(a, b, dims):
    return lax.dot_general(a, b, (dims, ((), ())), preferred_element_type=F32)


def swap(value):
    return lax.ppermute(value, "seq", swap_core())


def gather_z(block, after):
    z = lax.axis_index("cb")
    width = block.shape[1]
    pieces = [(0, block)] + [
        (k, lax.ppermute(block, "cb", shift_z(k))) for k in (4, 3, -3, 2, -2, 1, -1)
    ]
    full, after = together(jnp.zeros((block.shape[0], NZ * width), block.dtype), after)
    for k, piece in pieces:
        full = lax.dynamic_update_slice(full, piece, (0, ((z - k) % NZ) * width))
    return full, after


def weight_grad_body(places, order, a_here, a_there, b_here, b_there, *outs):
    block = outs[0].shape[0]
    for j, out in enumerate(outs):
        here, there = places
        tile = dot(columns(a_here, here, order[j], block), b_here[...], ((0,), (0,)))
        tile += dot(columns(a_there, there, order[j], block), b_there[...], ((0,), (0,)))
        out[...] = tile.astype(out.dtype)


def columns(ref, place, index, block):
    stride, step, size = place
    pieces = [
        ref[:, pl.ds(pl.multiple_of(index * stride + k * step, 128), size)]
        for k in range(block // size)
    ]
    return pieces[0] if len(pieces) == 1 else jnp.concatenate(pieces, axis=1)


def weight_grad(order, a_here, a_there, b_here, b_there, places):
    n_rows, width = b_here.shape
    deep = a_there.shape[1]
    block = deep // 4
    whole = pl.BlockSpec(memory_space=pltpu.VMEM)
    return pl.pallas_call(
        functools.partial(weight_grad_body, places),
        out_shape=[jax.ShapeDtypeStruct((block, width), t) for t in (BF, BF, F32, F32)],
        in_specs=[pl.BlockSpec(memory_space=pltpu.SMEM)] + [whole] * 4,
        out_specs=[whole] * 4,
        compiler_params=pltpu.CompilerParams(vmem_limit_bytes=VMEM_LIMIT),
        cost_estimate=pl.CostEstimate(
            flops=4 * n_rows * deep * width, bytes_accessed=8 << 20, transcendentals=0
        ),
        name="weight_grad",
    )(order, a_here, a_there, b_here, b_there)


def send_order(here, c, count):
    way = 1 - 2 * c
    return jnp.stack(
        [(here + 2) % count, (here - way) % count, (here + way) % count, here]
    ).astype(jnp.int32)


def first_stage(blocks, lane):
    relay, against, along, mine = blocks
    passing = lax.ppermute(relay, "seq", lane(1))
    direct = lax.ppermute(against, "seq", lane(-1))
    merged = (along + passing.astype(F32)).astype(BF)
    last = lax.ppermute(merged, "seq", lane(1))
    return mine + direct.astype(F32) + last.astype(F32)


def split_rows(row):
    high = lax.reduce_precision(row, 8, 7)
    middle = lax.reduce_precision(row - high, 8, 7)
    low = row - high - middle
    shape = (EXTRA, row.shape[1])
    at = lax.broadcasted_iota(jnp.int32, shape, 0)
    out = jnp.where(at == 0, high, jnp.where(at == 1, middle, jnp.where(at == 2, low, 0.0)))
    return out.astype(BF)


def read_rows(block, start):
    return jnp.sum(block[start : start + 3].astype(F32), axis=0, keepdims=True)


def head_swap(term, c):
    width = term.shape[1]
    blocks = jnp.moveaxis(term.reshape(NX, NY, NC, -1, width), 2, 0)
    other = lax.dynamic_index_in_dim(blocks, 1 - c, 0, keepdims=False)
    return swap(jnp.moveaxis(other, 1, 0))


def head_blocks(term, other, c, y):
    width = term.shape[1]
    blocks = term.reshape(NX, NY, NC, -1, width)
    rows = blocks.shape[3]
    way = 1 - 2 * c

    def at(index):
        index = index % NY
        mine = lax.dynamic_slice(blocks, (0, index, c, 0, 0), (NX, 1, 1, rows, width))
        more = lax.dynamic_index_in_dim(other, index, 0, keepdims=False)
        total = mine.reshape(NX, rows, width).astype(F32) + more.astype(F32)
        return total.reshape(NX * rows, width)

    return (at(y + 2).astype(BF), at(y - way).astype(BF), at(y + way), at(y))


def second_stage(part, here, count, shift, value):
    width = part.shape[1]
    blocks = part.reshape(count, -1, width)
    rows = blocks.shape[1]
    total = lax.dynamic_index_in_dim(blocks, here, 0, keepdims=False)
    extra = split_rows(value)
    for k in (2, 1, 3):
        piece = lax.dynamic_index_in_dim(blocks, (here + k) % count, 0, keepdims=False)
        piece = jnp.concatenate([piece.astype(BF), extra], axis=0)
        piece = lax.ppermute(piece, "seq", shift(k))
        total = total + piece[:rows].astype(F32)
        value = value + read_rows(piece, rows)
    return total, value


def local(context, lengths, tokens, masks, w_in, w_head):
    seq_count = lax.axis_size("seq")
    cb_total = lax.axis_size("cb") * w_in.shape[0]
    seq_here = lax.axis_index("seq")
    c, y, x = seq_here % NC, (seq_here // NC) % NY, seq_here // (NC * NY)
    rows_here = context.shape[0]
    streams_here = rows_here // FRAMES
    w_rows, width = w_in.shape[1:]
    vocab = w_rows * seq_count

    pair = lax.all_gather(jnp.concatenate([w_in[0], w_head[0]], axis=1), "seq", axis=0, tiled=True)

    positions = jnp.arange(rows_here, dtype=jnp.int32)
    own_stream = seq_here * streams_here + positions // FRAMES
    live = positions % FRAMES < lookup(lengths, own_stream)
    keeps = live & (masks[:, 0] > 0)
    keep_float = keeps.astype(F32)
    labels = jnp.where(keeps, tokens[:, 0], -1)
    tally = jnp.concatenate([keep_float, jnp.zeros((1024 - rows_here,), F32)]).reshape(8, 128)
    count = jnp.sum(lax.all_gather(tally, "seq", axis=0))
    rows_total = FRAMES * streams_here * seq_count
    weight = keep_float * (rows_total / (count * cb_total))

    full_rows, weight = gather_z(context, weight)
    by_core = full_rows.reshape(rows_here, NX * NY, NC, w_rows)
    even = by_core[:, :, 0].reshape(rows_here, -1)
    odd = by_core[:, :, 1].reshape(rows_here, -1)
    rows_keep = jnp.where(c == 0, even, odd)
    rows_other = swap(jnp.where(c == 0, odd, even))
    full_rows, weight, rows_keep, rows_other, pair = together(
        full_rows, weight, rows_keep, rows_other, pair
    )
    in_matrix = pair[:, :width]
    head_matrix = pair[:, width:]

    hidden = dot(full_rows, in_matrix, ((1,), (0,)))
    inverse = lax.rsqrt(jnp.mean(hidden * hidden, axis=1, keepdims=True) + EPS)
    normed = hidden * inverse
    normed_bf = normed.astype(BF)
    logits = dot(normed_bf, head_matrix, ((1,), (1,)))
    peak = jnp.max(logits, axis=1, keepdims=True)
    shifted = jnp.exp(logits - peak)
    total = jnp.sum(shifted, axis=1, keepdims=True)
    vocab_ids = jnp.arange(vocab, dtype=jnp.int32)
    target = vocab_ids[None, :] == labels[:, None]
    picked = jnp.sum(jnp.where(target, logits, 0.0), axis=1)
    entropy_terms = jnp.where(keeps, peak[:, 0] + jnp.log(total[:, 0]) - picked, 0.0)
    grad_logits = ((shifted / total - target.astype(F32)) * weight[:, None]).astype(BF)
    head_term = dot(grad_logits, normed_bf, ((0,), (0,))).astype(BF)
    head_other = head_swap(head_term, c)
    spread = lax.broadcasted_iota(jnp.int32, (rows_here, width), 1)
    spread = spread == lax.broadcasted_iota(jnp.int32, (rows_here, width), 0)
    row = jnp.sum(jnp.where(spread, entropy_terms[:, None], 0.0), axis=0, keepdims=True)
    row = row / (count * cb_total)
    row_in = swap(row)
    grad_normed = dot(grad_logits, head_matrix, ((1,), (0,)))
    grad_hidden = inverse * (
        grad_normed - normed * jnp.mean(grad_normed * normed, axis=1, keepdims=True)
    )
    grad_hidden = grad_hidden.astype(BF)
    grad_hidden, row, row_in = together(grad_hidden, row, row_in)
    hidden_other = swap(grad_hidden)
    row = row + row_in
    row_in = lax.ppermute(row, "cb", shift_z(1))
    context_term = dot(grad_hidden, in_matrix, ((1,), (1,))).astype(BF)
    head_other, context_term, row, row_in = together(head_other, context_term, row, row_in)
    context_part = lax.psum_scatter(context_term, "cb", scatter_dimension=1, tiled=True)
    row = row + row_in
    row_in = lax.ppermute(row, "cb", shift_z(2))
    head_parts = head_blocks(head_term, head_other, c, y)
    head_parts, hidden_other, row, row_in = together(head_parts, hidden_other, row, row_in)
    row = row + row_in
    row_in = lax.ppermute(row, "cb", shift_z(4))
    half = vocab // 2
    block_rows = half // NX
    in_parts = weight_grad(
        send_order(x, c, NX), rows_keep, rows_other, grad_hidden, hidden_other,
        ((block_rows, block_rows, block_rows),) * 2,
    )
    in_parts, row, row_in = together(in_parts, row, row_in)
    loss = row + row_in
    head_sum = first_stage(head_parts, lane_y)
    in_sum = first_stage(in_parts, lane_x)
    head_part, loss = second_stage(head_sum, x, NX, shift_x, loss)
    in_part, loss = second_stage(in_sum, y, NY, shift_y, loss)
    return (jnp.sum(loss), context_part, in_part[None], head_part[None])


def solution(mesh):
    in_specs = (
        P("seq", "cb"),
        P(),
        P("seq", "cb"),
        P("seq", "cb"),
        P("cb", "seq", None),
        P("cb", "seq", None),
    )
    out_specs = (P(), P("seq", "cb"), P("cb", "seq", None), P("cb", "seq", None))
    return jax.shard_map(local, mesh=mesh, in_specs=in_specs, out_specs=out_specs, check_vma=False)
```

```python
import functools

import jax
import jax.numpy as jnp
from jax import lax
from jax.experimental import pallas as pl
from jax.experimental.pallas import tpu as pltpu
from jax.sharding import PartitionSpec as P

FRAMES = 256
EPS = 1e-06
BF = jnp.bfloat16
F32 = jnp.float32
NX, NY, NC, NZ = 4, 4, 2, 8
EXTRA = 16
VMEM_LIMIT = 20 * 1024 * 1024


def seq_index(x, y, c):
    return (x * NY + y) * NC + c


def moves(step):
    pairs = []
    for x in range(NX):
        for y in range(NY):
            for c in range(NC):
                to_x, to_y, to_c = step(x, y, c)
                pairs.append((seq_index(x, y, c), seq_index(to_x % NX, to_y % NY, to_c)))
    return pairs


def shift_x(k):
    return moves(lambda x, y, c: (x + k, y, c))


def shift_y(k):
    return moves(lambda x, y, c: (x, y + k, c))


def lane_x(k):
    return moves(lambda x, y, c: (x + k * (1 - 2 * c), y, c))


def lane_y(k):
    return moves(lambda x, y, c: (x, y + k * (1 - 2 * c), c))


def swap_core():
    return moves(lambda x, y, c: (x, y, 1 - c))


def shift_z(k):
    return [(i, (i + k) % NZ) for i in range(NZ)]


def lookup(table, index):
    spots = jnp.arange(table.shape[0], dtype=jnp.int32)
    return jnp.sum(jnp.where(index[:, None] == spots[None, :], table[None, :], 0), axis=1)


def together(*values):
    return lax.optimization_barrier(values)


def dot(a, b, dims):
    return lax.dot_general(a, b, (dims, ((), ())), preferred_element_type=F32)


def swap(value):
    return lax.ppermute(value, "seq", swap_core())


def gather_inputs(block, shard, c, y, x):
    z = lax.axis_index("cb")
    rows, width = shard.shape
    slab = block.shape[1]
    kind = slab // NC
    full = jnp.zeros((block.shape[0], NZ * slab), block.dtype)
    other = jnp.zeros((block.shape[0], NZ * kind), block.dtype)

    def put_slab(full, other, piece, k):
        at = (z - k) % NZ
        full = lax.dynamic_update_slice(full, piece, (0, at * slab))
        return full, lax.dynamic_update_slice(other, piece[:, kind:], (0, at * kind))

    full, other = put_slab(full, other, block, 0)
    line = jnp.zeros((NY, rows, width), BF)
    line = lax.dynamic_update_slice(line, shard[None], (y, 0, 0))
    got = [lax.ppermute(shard, "seq", shift_y(k)) for k in (2, 1, 3)]
    up = lax.ppermute(block, "cb", shift_z(1))
    down = lax.ppermute(block, "cb", shift_z(-1))
    got = together(*got)
    for k, piece in zip((2, 1, 3), got):
        line = lax.dynamic_update_slice(line, piece[None], ((y - k) % NY, 0, 0))
    above = lax.ppermute(line, "seq", shift_x(1))
    below = lax.ppermute(line, "seq", shift_x(-1))
    for k in (1, 2, 3):
        full, other = put_slab(full, other, up, k)
        full, other = put_slab(full, other, down, -k)
        up = lax.ppermute(up, "cb", shift_z(1))
        if k < 3:
            down = lax.ppermute(down, "cb", shift_z(-1))
            up, down = together(up, down)
    full, other = put_slab(full, other, up, 4)
    far = lax.ppermute(jnp.where(c == 0, above, below), "seq", lane_x(1))
    weight = jnp.zeros((NX, NY // 2, NC, 2 * rows, width), BF)
    for piece, k in ((line, 0), (above, -1), (below, 1), (far, 2)):
        for part, half in enumerate((piece, swap(piece))):
            half = half.reshape(1, NY // 2, 1, 2 * rows, width)
            weight = lax.dynamic_update_slice(weight, half, ((x + k) % NX, 0, part, 0, 0))
    return full, other, weight.reshape(-1, width)


def weight_grad_body(places, order, a_here, a_there, b_here, b_there, *outs):
    block = outs[0].shape[0]
    for j, out in enumerate(outs):
        here, there = places
        tile = dot(columns(a_here, here, order[j], block), b_here[...], ((0,), (0,)))
        tile += dot(columns(a_there, there, order[j], block), b_there[...], ((0,), (0,)))
        out[...] = tile.astype(out.dtype)


def columns(ref, place, index, block):
    stride, step, size = place
    pieces = [
        ref[:, pl.ds(pl.multiple_of(index * stride + k * step, 128), size)]
        for k in range(block // size)
    ]
    return pieces[0] if len(pieces) == 1 else jnp.concatenate(pieces, axis=1)


def weight_grad(order, a_here, a_there, b_here, b_there, places):
    n_rows, width = b_here.shape
    deep = a_there.shape[1]
    block = deep // 4
    whole = pl.BlockSpec(memory_space=pltpu.VMEM)
    return pl.pallas_call(
        functools.partial(weight_grad_body, places),
        out_shape=[jax.ShapeDtypeStruct((block, width), t) for t in (BF, BF, F32, F32)],
        in_specs=[pl.BlockSpec(memory_space=pltpu.SMEM)] + [whole] * 4,
        out_specs=[whole] * 4,
        compiler_params=pltpu.CompilerParams(vmem_limit_bytes=VMEM_LIMIT),
        cost_estimate=pl.CostEstimate(
            flops=4 * n_rows * deep * width, bytes_accessed=8 << 20, transcendentals=0
        ),
        name="weight_grad",
    )(order, a_here, a_there, b_here, b_there)


def send_order(here, c, count):
    way = 1 - 2 * c
    return jnp.stack(
        [(here + 2) % count, (here - way) % count, (here + way) % count, here]
    ).astype(jnp.int32)


def first_stage(blocks, lane):
    relay, against, along, mine = blocks
    passing = lax.ppermute(relay, "seq", lane(1))
    direct = lax.ppermute(against, "seq", lane(-1))
    merged = (along + passing.astype(F32)).astype(BF)
    last = lax.ppermute(merged, "seq", lane(1))
    return mine + direct.astype(F32) + last.astype(F32)


def split_rows(row):
    high = lax.reduce_precision(row, 8, 7)
    middle = lax.reduce_precision(row - high, 8, 7)
    low = row - high - middle
    shape = (EXTRA, row.shape[1])
    at = lax.broadcasted_iota(jnp.int32, shape, 0)
    out = jnp.where(at == 0, high, jnp.where(at == 1, middle, jnp.where(at == 2, low, 0.0)))
    return out.astype(BF)


def read_rows(block, start):
    return jnp.sum(block[start : start + 3].astype(F32), axis=0, keepdims=True)


def head_swap(term, c):
    width = term.shape[1]
    blocks = jnp.moveaxis(term.reshape(NX, NY, NC, -1, width), 2, 0)
    other = lax.dynamic_index_in_dim(blocks, 1 - c, 0, keepdims=False)
    return swap(jnp.moveaxis(other, 1, 0))


def head_blocks(term, other, c, y):
    width = term.shape[1]
    blocks = term.reshape(NX, NY, NC, -1, width)
    rows = blocks.shape[3]
    way = 1 - 2 * c

    def at(index):
        index = index % NY
        mine = lax.dynamic_slice(blocks, (0, index, c, 0, 0), (NX, 1, 1, rows, width))
        more = lax.dynamic_index_in_dim(other, index, 0, keepdims=False)
        total = mine.reshape(NX, rows, width).astype(F32) + more.astype(F32)
        return total.reshape(NX * rows, width)

    return (at(y + 2).astype(BF), at(y - way).astype(BF), at(y + way), at(y))


def second_stage(part, here, count, shift, value, beside=None):
    width = part.shape[1]
    blocks = part.reshape(count, -1, width)
    rows = blocks.shape[1]
    total = lax.dynamic_index_in_dim(blocks, here, 0, keepdims=False)
    extra = split_rows(value)
    pieces = []
    for k in (2, 1, 3):
        piece = lax.dynamic_index_in_dim(blocks, (here + k) % count, 0, keepdims=False)
        piece = jnp.concatenate([piece.astype(BF), extra], axis=0)
        pieces.append(lax.ppermute(piece, "seq", shift(k)))
    if beside is not None:
        *pieces, beside = together(*pieces, beside)
    for piece in pieces:
        total = total + piece[:rows].astype(F32)
        value = value + read_rows(piece, rows)
    return total, value, beside


def local(context, lengths, tokens, masks, w_in, w_head):
    head_matrix = lax.all_gather(w_head[0], "seq", axis=0, tiled=True)
    seq_count = lax.axis_size("seq")
    cb_total = lax.axis_size("cb") * w_in.shape[0]
    seq_here = lax.axis_index("seq")
    c, y, x = seq_here % NC, (seq_here // NC) % NY, seq_here // (NC * NY)
    rows_here = context.shape[0]
    streams_here = rows_here // FRAMES
    w_rows, width = w_in.shape[1:]
    vocab = w_rows * seq_count

    positions = jnp.arange(rows_here, dtype=jnp.int32)
    own_stream = seq_here * streams_here + positions // FRAMES
    live = positions % FRAMES < lookup(lengths, own_stream)
    keeps = live & (masks[:, 0] > 0)
    keep_float = keeps.astype(F32)
    flags = jnp.concatenate([keep_float, jnp.zeros((w_rows * 128 - rows_here,), F32)])
    flags = flags.reshape(w_rows, 128).astype(BF)
    in_shard = jnp.concatenate([w_in[0], flags], axis=1)

    slab = context.shape[1]
    by_core = context.reshape(rows_here, slab // (NC * w_rows), NC, w_rows)
    even = by_core[:, :, 0].reshape(rows_here, -1)
    odd = by_core[:, :, 1].reshape(rows_here, -1)
    block = jnp.concatenate([jnp.where(c == 0, even, odd), jnp.where(c == 0, odd, even)], axis=1)
    full_rows, rows_other, in_wide = gather_inputs(block, in_shard, c, y, x)

    labels = jnp.where(keeps, tokens[:, 0], -1)
    rows_other = swap(rows_other)
    rows_total = FRAMES * streams_here * seq_count
    count = jnp.sum(in_wide[:, width:].astype(F32))
    weight = keep_float * (rows_total / (count * cb_total))
    in_matrix = in_wide[:, :width]
    in_matrix, head_matrix = together(in_matrix, head_matrix)

    hidden = dot(full_rows, in_matrix, ((1,), (0,)))
    inverse = lax.rsqrt(jnp.mean(hidden * hidden, axis=1, keepdims=True) + EPS)
    normed = hidden * inverse
    normed_bf = normed.astype(BF)
    logits = dot(normed_bf, head_matrix, ((1,), (1,)))
    peak = jnp.max(logits, axis=1, keepdims=True)
    shifted = jnp.exp(logits - peak)
    total = jnp.sum(shifted, axis=1, keepdims=True)
    vocab_ids = jnp.arange(vocab, dtype=jnp.int32)
    target = vocab_ids[None, :] == labels[:, None]
    picked = jnp.sum(jnp.where(target, logits, 0.0), axis=1)
    entropy_terms = jnp.where(keeps, peak[:, 0] + jnp.log(total[:, 0]) - picked, 0.0)
    grad_logits = ((shifted / total - target.astype(F32)) * weight[:, None]).astype(BF)
    head_term = dot(grad_logits, normed_bf, ((0,), (0,))).astype(BF)
    head_other = head_swap(head_term, c)
    spread = lax.broadcasted_iota(jnp.int32, (rows_here, width), 1)
    spread = spread == lax.broadcasted_iota(jnp.int32, (rows_here, width), 0)
    row = jnp.sum(jnp.where(spread, entropy_terms[:, None], 0.0), axis=0, keepdims=True)
    row = row / (count * cb_total)
    row_in = swap(row)
    grad_normed = dot(grad_logits, head_matrix, ((1,), (0,)))
    grad_hidden = inverse * (
        grad_normed - normed * jnp.mean(grad_normed * normed, axis=1, keepdims=True)
    )
    grad_hidden = grad_hidden.astype(BF)
    grad_hidden, row, row_in = together(grad_hidden, row, row_in)
    hidden_other = swap(grad_hidden)
    row = row + row_in
    row_in = lax.ppermute(row, "cb", shift_z(1))
    context_term = dot(grad_hidden, in_matrix, ((1,), (1,))).astype(BF)
    head_other, context_term, row, row_in = together(head_other, context_term, row, row_in)
    context_part = lax.psum_scatter(context_term, "cb", scatter_dimension=1, tiled=True)
    row = row + row_in
    row_in = lax.ppermute(row, "cb", shift_z(2))
    head_parts = head_blocks(head_term, head_other, c, y)
    head_parts, hidden_other = together(head_parts, hidden_other)
    piece = slab // NC
    in_parts = weight_grad(
        send_order(x, c, NX), full_rows, rows_other, grad_hidden, hidden_other,
        ((2 * slab, slab, piece), (2 * piece, piece, piece)),
    )
    in_parts, row, row_in = together(in_parts, row, row_in)
    row = row + row_in
    head_passing = lax.ppermute(head_parts[0], "seq", lane_y(1))
    head_direct = lax.ppermute(head_parts[1], "seq", lane_y(-1))
    head_passing, row = together(head_passing, row)
    loss = row + lax.ppermute(row, "cb", shift_z(4))
    head_merged = (head_parts[2] + head_passing.astype(F32)).astype(BF)
    head_last = lax.ppermute(head_merged, "seq", lane_y(1))
    head_sum = head_parts[3] + head_direct.astype(F32) + head_last.astype(F32)
    in_sum = first_stage(in_parts, lane_x)
    own = context_part[:, :piece].reshape(rows_here, -1, 1, w_rows)
    rest = context_part[:, piece:].reshape(rows_here, -1, 1, w_rows)
    ordered = jnp.concatenate(
        [jnp.where(c == 0, own, rest), jnp.where(c == 0, rest, own)], axis=2
    ).reshape(rows_here, slab)
    head_part, loss, _ = second_stage(head_sum, x, NX, shift_x, loss)
    in_part, loss, ordered = second_stage(in_sum, y, NY, shift_y, loss, ordered)
    return (jnp.sum(loss), ordered, in_part[None], head_part[None])


def solution(mesh):
    in_specs = (
        P("seq", "cb"),
        P(),
        P("seq", "cb"),
        P("seq", "cb"),
        P("cb", "seq", None),
        P("cb", "seq", None),
    )
    out_specs = (P(), P("seq", "cb"), P("cb", "seq", None), P("cb", "seq", None))
    return jax.shard_map(local, mesh=mesh, in_specs=in_specs, out_specs=out_specs, check_vma=False)
```

```python
import functools

import jax
import jax.numpy as jnp
from jax import lax
from jax.experimental import pallas as pl
from jax.experimental.pallas import tpu as pltpu
from jax.sharding import PartitionSpec as P

FRAMES = 256
EPS = 1e-06
BF = jnp.bfloat16
F32 = jnp.float32
NX, NY, NC, NZ = 4, 4, 2, 8
EXTRA = 16
VMEM_LIMIT = 20 * 1024 * 1024


def seq_index(x, y, c):
    return (x * NY + y) * NC + c


def moves(step):
    pairs = []
    for x in range(NX):
        for y in range(NY):
            for c in range(NC):
                to_x, to_y, to_c = step(x, y, c)
                pairs.append((seq_index(x, y, c), seq_index(to_x % NX, to_y % NY, to_c)))
    return pairs


def shift_x(k):
    return moves(lambda x, y, c: (x + k, y, c))


def shift_y(k):
    return moves(lambda x, y, c: (x, y + k, c))


def lane_x(k):
    return moves(lambda x, y, c: (x + k * (1 - 2 * c), y, c))


def lane_y(k):
    return moves(lambda x, y, c: (x, y + k * (1 - 2 * c), c))


def swap_core():
    return moves(lambda x, y, c: (x, y, 1 - c))


def shift_z(k):
    return [(i, (i + k) % NZ) for i in range(NZ)]


def lookup(table, index):
    spots = jnp.arange(table.shape[0], dtype=jnp.int32)
    return jnp.sum(jnp.where(index[:, None] == spots[None, :], table[None, :], 0), axis=1)


def together(*values):
    return lax.optimization_barrier(values)


def dot(a, b, dims):
    return lax.dot_general(a, b, (dims, ((), ())), preferred_element_type=F32)


def swap(value):
    return lax.ppermute(value, "seq", swap_core())


def gather_inputs(block, shard, c, y, x):
    z = lax.axis_index("cb")
    rows, width = shard.shape
    slab = block.shape[1]
    kind = slab // NC
    full = jnp.zeros((block.shape[0], NZ * slab), block.dtype)
    other = jnp.zeros((block.shape[0], NZ * kind), block.dtype)

    def put_slab(full, other, piece, k):
        at = (z - k) % NZ
        full = lax.dynamic_update_slice(full, piece, (0, at * slab))
        return full, lax.dynamic_update_slice(other, piece[:, kind:], (0, at * kind))

    full, other = put_slab(full, other, block, 0)
    line = jnp.zeros((NY, rows, width), BF)
    line = lax.dynamic_update_slice(line, shard[None], (y, 0, 0))
    got = [lax.ppermute(shard, "seq", shift_y(k)) for k in (2, 1, 3)]
    up = lax.ppermute(block, "cb", shift_z(1))
    down = lax.ppermute(block, "cb", shift_z(-1))
    got = together(*got)
    for k, piece in zip((2, 1, 3), got):
        line = lax.dynamic_update_slice(line, piece[None], ((y - k) % NY, 0, 0))
    above = lax.ppermute(line, "seq", shift_x(1))
    below = lax.ppermute(line, "seq", shift_x(-1))
    for k in (1, 2, 3):
        full, other = put_slab(full, other, up, k)
        full, other = put_slab(full, other, down, -k)
        up = lax.ppermute(up, "cb", shift_z(1))
        if k < 3:
            down = lax.ppermute(down, "cb", shift_z(-1))
            up, down = together(up, down)
    full, other = put_slab(full, other, up, 4)
    far = lax.ppermute(jnp.where(c == 0, above, below), "seq", lane_x(1))
    weight = jnp.zeros((NX, NY // 2, NC, 2 * rows, width), BF)
    for piece, k in ((line, 0), (above, -1), (below, 1), (far, 2)):
        for part, half in enumerate((piece, swap(piece))):
            half = half.reshape(1, NY // 2, 1, 2 * rows, width)
            weight = lax.dynamic_update_slice(weight, half, ((x + k) % NX, 0, part, 0, 0))
    return full, other, weight.reshape(-1, width)


def weight_grad_body(places, order, a_here, a_there, b_here, b_there, *outs):
    block = outs[0].shape[0]
    for j, out in enumerate(outs):
        here, there = places
        tile = dot(columns(a_here, here, order[j], block), b_here[...], ((0,), (0,)))
        tile += dot(columns(a_there, there, order[j], block), b_there[...], ((0,), (0,)))
        out[...] = tile.astype(out.dtype)


def columns(ref, place, index, block):
    stride, step, size = place
    pieces = [
        ref[:, pl.ds(pl.multiple_of(index * stride + k * step, 128), size)]
        for k in range(block // size)
    ]
    return pieces[0] if len(pieces) == 1 else jnp.concatenate(pieces, axis=1)


def weight_grad(order, a_here, a_there, b_here, b_there, places):
    n_rows, width = b_here.shape
    deep = a_there.shape[1]
    block = deep // 4
    whole = pl.BlockSpec(memory_space=pltpu.VMEM)
    return pl.pallas_call(
        functools.partial(weight_grad_body, places),
        out_shape=[jax.ShapeDtypeStruct((block, width), t) for t in (BF, BF, F32, F32)],
        in_specs=[pl.BlockSpec(memory_space=pltpu.SMEM)] + [whole] * 4,
        out_specs=[whole] * 4,
        compiler_params=pltpu.CompilerParams(vmem_limit_bytes=VMEM_LIMIT),
        cost_estimate=pl.CostEstimate(
            flops=4 * n_rows * deep * width, bytes_accessed=8 << 20, transcendentals=0
        ),
        name="weight_grad",
    )(order, a_here, a_there, b_here, b_there)


def send_order(here, c, count):
    way = 1 - 2 * c
    return jnp.stack(
        [(here + 2) % count, (here - way) % count, (here + way) % count, here]
    ).astype(jnp.int32)


def first_stage(blocks, lane):
    relay, against, along, mine = blocks
    passing = lax.ppermute(relay, "seq", lane(1))
    direct = lax.ppermute(against, "seq", lane(-1))
    merged = (along + passing.astype(F32)).astype(BF)
    last = lax.ppermute(merged, "seq", lane(1))
    return mine + direct.astype(F32) + last.astype(F32)


def split_rows(row):
    high = lax.reduce_precision(row, 8, 7)
    middle = lax.reduce_precision(row - high, 8, 7)
    low = row - high - middle
    shape = (EXTRA, row.shape[1])
    at = lax.broadcasted_iota(jnp.int32, shape, 0)
    out = jnp.where(at == 0, high, jnp.where(at == 1, middle, jnp.where(at == 2, low, 0.0)))
    return out.astype(BF)


def read_rows(block, start):
    return jnp.sum(block[start : start + 3].astype(F32), axis=0, keepdims=True)


def head_swap(term, c):
    width = term.shape[1]
    blocks = jnp.moveaxis(term.reshape(NX, NY, NC, -1, width), 2, 0)
    other = lax.dynamic_index_in_dim(blocks, 1 - c, 0, keepdims=False)
    return swap(jnp.moveaxis(other, 1, 0))


def head_blocks(term, other, c, y):
    width = term.shape[1]
    blocks = term.reshape(NX, NY, NC, -1, width)
    rows = blocks.shape[3]
    way = 1 - 2 * c

    def at(index):
        index = index % NY
        mine = lax.dynamic_slice(blocks, (0, index, c, 0, 0), (NX, 1, 1, rows, width))
        more = lax.dynamic_index_in_dim(other, index, 0, keepdims=False)
        total = mine.reshape(NX, rows, width).astype(F32) + more.astype(F32)
        return total.reshape(NX * rows, width)

    return (at(y + 2).astype(BF), at(y - way).astype(BF), at(y + way), at(y))


def second_stage(part, here, count, shift, value, beside=None):
    width = part.shape[1]
    blocks = part.reshape(count, -1, width)
    rows = blocks.shape[1]
    total = lax.dynamic_index_in_dim(blocks, here, 0, keepdims=False)
    extra = split_rows(value)
    pieces = []
    for k in (2, 1, 3):
        piece = lax.dynamic_index_in_dim(blocks, (here + k) % count, 0, keepdims=False)
        piece = jnp.concatenate([piece.astype(BF), extra], axis=0)
        pieces.append(lax.ppermute(piece, "seq", shift(k)))
    if beside is not None:
        *pieces, beside = together(*pieces, beside)
    for piece in pieces:
        total = total + piece[:rows].astype(F32)
        value = value + read_rows(piece, rows)
    return total, value, beside


def local(context, lengths, tokens, masks, w_in, w_head):
    head_matrix = lax.all_gather(w_head[0], "seq", axis=0, tiled=True)
    seq_count = lax.axis_size("seq")
    cb_total = lax.axis_size("cb") * w_in.shape[0]
    seq_here = lax.axis_index("seq")
    c, y, x = seq_here % NC, (seq_here // NC) % NY, seq_here // (NC * NY)
    rows_here = context.shape[0]
    streams_here = rows_here // FRAMES
    w_rows, width = w_in.shape[1:]
    vocab = w_rows * seq_count

    positions = jnp.arange(rows_here, dtype=jnp.int32)
    own_stream = seq_here * streams_here + positions // FRAMES
    live = positions % FRAMES < lookup(lengths, own_stream)
    keeps = live & (masks[:, 0] > 0)
    keep_float = keeps.astype(F32)
    flags = jnp.concatenate([keep_float, jnp.zeros((w_rows * 128 - rows_here,), F32)])
    flags = flags.reshape(w_rows, 128).astype(BF)
    in_shard = jnp.concatenate([w_in[0], flags], axis=1)

    slab = context.shape[1]
    by_core = context.reshape(rows_here, slab // (NC * w_rows), NC, w_rows)
    even = by_core[:, :, 0].reshape(rows_here, -1)
    odd = by_core[:, :, 1].reshape(rows_here, -1)
    block = jnp.concatenate([jnp.where(c == 0, even, odd), jnp.where(c == 0, odd, even)], axis=1)
    full_rows, rows_other, in_wide = gather_inputs(block, in_shard, c, y, x)

    labels = jnp.where(keeps, tokens[:, 0], -1)
    rows_other = swap(rows_other)
    rows_total = FRAMES * streams_here * seq_count
    count = jnp.sum(in_wide[:, width:].astype(F32))
    weight = keep_float * (rows_total / (count * cb_total))
    in_matrix = in_wide[:, :width]
    weight, in_matrix = together(weight, in_matrix)

    hidden = dot(full_rows, in_matrix, ((1,), (0,)))
    inverse = lax.rsqrt(jnp.mean(hidden * hidden, axis=1, keepdims=True) + EPS)
    normed = hidden * inverse
    normed_bf = normed.astype(BF)
    logits = dot(normed_bf, head_matrix, ((1,), (1,)))
    peak = jnp.max(logits, axis=1, keepdims=True)
    shifted = jnp.exp(logits - peak)
    total = jnp.sum(shifted, axis=1, keepdims=True)
    vocab_ids = jnp.arange(vocab, dtype=jnp.int32)
    target = vocab_ids[None, :] == labels[:, None]
    picked = jnp.sum(jnp.where(target, logits, 0.0), axis=1)
    entropy_terms = jnp.where(keeps, peak[:, 0] + jnp.log(total[:, 0]) - picked, 0.0)
    grad_logits = ((shifted / total - target.astype(F32)) * weight[:, None]).astype(BF)
    head_term = dot(grad_logits, normed_bf, ((0,), (0,))).astype(BF)
    head_other = head_swap(head_term, c)
    spread = lax.broadcasted_iota(jnp.int32, (rows_here, width), 1)
    spread = spread == lax.broadcasted_iota(jnp.int32, (rows_here, width), 0)
    row = jnp.sum(jnp.where(spread, entropy_terms[:, None], 0.0), axis=0, keepdims=True)
    row = row / (count * cb_total)
    row_in = swap(row)
    grad_normed = dot(grad_logits, head_matrix, ((1,), (0,)))
    grad_hidden = inverse * (
        grad_normed - normed * jnp.mean(grad_normed * normed, axis=1, keepdims=True)
    )
    grad_hidden = grad_hidden.astype(BF)
    grad_hidden, row, row_in = together(grad_hidden, row, row_in)
    hidden_other = swap(grad_hidden)
    row = row + row_in
    row_in = lax.ppermute(row, "cb", shift_z(1))
    context_term = dot(grad_hidden, in_matrix, ((1,), (1,))).astype(BF)
    head_other, context_term, row, row_in = together(head_other, context_term, row, row_in)
    context_part = lax.psum_scatter(context_term, "cb", scatter_dimension=1, tiled=True)
    row = row + row_in
    row_in = lax.ppermute(row, "cb", shift_z(2))
    head_parts = head_blocks(head_term, head_other, c, y)
    head_parts, hidden_other, row, row_in = together(head_parts, hidden_other, row, row_in)
    row = row + row_in
    row_in = lax.ppermute(row, "cb", shift_z(4))
    piece = slab // NC
    in_parts = weight_grad(
        send_order(x, c, NX), full_rows, rows_other, grad_hidden, hidden_other,
        ((2 * slab, slab, piece), (2 * piece, piece, piece)),
    )
    in_parts, row, row_in = together(in_parts, row, row_in)
    loss = row + row_in
    head_sum = first_stage(head_parts, lane_y)
    in_sum = first_stage(in_parts, lane_x)
    own = context_part[:, :piece].reshape(rows_here, -1, 1, w_rows)
    rest = context_part[:, piece:].reshape(rows_here, -1, 1, w_rows)
    ordered = jnp.concatenate(
        [jnp.where(c == 0, own, rest), jnp.where(c == 0, rest, own)], axis=2
    ).reshape(rows_here, slab)
    head_part, loss, _ = second_stage(head_sum, x, NX, shift_x, loss)
    in_part, loss, ordered = second_stage(in_sum, y, NY, shift_y, loss, ordered)
    return (jnp.sum(loss), ordered, in_part[None], head_part[None])


def solution(mesh):
    in_specs = (
        P("seq", "cb"),
        P(),
        P("seq", "cb"),
        P("seq", "cb"),
        P("cb", "seq", None),
        P("cb", "seq", None),
    )
    out_specs = (P(), P("seq", "cb"), P("cb", "seq", None), P("cb", "seq", None))
    return jax.shard_map(local, mesh=mesh, in_specs=in_specs, out_specs=out_specs, check_vma=False)
```
